256 devices in a mesh: inst: 16 (over z, x_hi), head: 16 (over x_lo, y, core).
Axes of the slice: x: 4 (x_hi: 2, x_lo: 2; x = x_hi * 2 + x_lo), y: 4, z: 8, core: 2. Of those that a mesh axis runs over, the one named last changes fastest.
Arguments:
- queries: bfloat16 [16, 128, 128], P('inst', 'head'), may hold values from -6 to 6
- page_pool: bfloat16 [4352, 2, 16, 64, 128], P('inst', None, 'head'), may hold values from -6 to 6, as said below
- block_tables: int32 [16, 16, 16], P(None, 'inst'), may hold values from 0 to 271, as said below
- token_counts: int32 [16, 16], P(None, 'inst'), may hold values from 1 to 1024, as said below
- move_slots: int32 [16, 32], P('inst'), may hold values from 0 to 271, as said below
- out_weight: bfloat16 [16384, 16384], P('head', 'inst'), may hold values from -0.046875 to 0.046875
Outputs:
- projected: bfloat16 [16, 16384], P('head', 'inst')
- arrived: bfloat16 [512, 2, 16, 64, 128], P('inst', None, 'head')
The draws below stay inside these ranges and needn't reach their ends.
Inputs may be any that keep to these rules, and one draw needn't show every extreme that they name: `block_tables`: in each instance the slots of all requests and pages are distinct. `token_counts`: every request has 1024 tokens on some instance. `move_slots`: distinct within each instance. `page_pool`: stored heads c and c2 are equal wherever c * 8 // 16 == c2 * 8 // 16: copies of one key-value head of the model.
All inputs are finite; a program needn't handle non-finite values.
Results may differ from the reference program's by a relative error of at most 0.007.
Values may be sent and summed in bfloat16 or wider, within the bound.
No kernel may reach another device: no remote copies, remote signals or barrier semaphores. Data moves between devices by JAX's collectives and lax.ppermute only.
A program may use at most 128 MiB of HBM per device.

```python
import jax
import jax.numpy as jnp
from jax import lax

D = 16384
QH = 128
KVH = 8
HD = 128
REQ = 16
PAGE = 64
PPI = 16
MOVES = 32
KVS = 16
SLOTS = 272
N_INST = 16


def draw_queries(key, part):
    key = jax.random.fold_in(key, 11)
    first = jax.random.fold_in(key, 0)
    values = jnp.clip(jax.random.normal(first, (REQ, QH, HD), jnp.float32), -6.0, 6.0)
    return values.astype(jnp.bfloat16)


def draw_page_pool(key, part):
    key = jax.random.fold_in(key, 13)
    first = jax.random.fold_in(key, 0)
    shape = (N_INST * SLOTS, 2, KVH, PAGE, HD)
    values = jnp.clip(jax.random.normal(first, shape, jnp.float32), -6.0, 6.0)
    values = jnp.repeat(values, KVS // KVH, axis=2)
    return values.astype(jnp.bfloat16)


def draw_block_tables(key, part):
    key = jax.random.fold_in(key, 21)
    inst_keys = jax.random.split(key, N_INST)
    chosen = jax.vmap(lambda sub: jax.random.permutation(sub, SLOTS)[:REQ * PPI])(inst_keys)
    return jnp.transpose(chosen.reshape(N_INST, REQ, PPI), (1, 0, 2)).astype(jnp.int32)


def draw_token_counts(key, part):
    key = jax.random.fold_in(key, 31)
    first, second, third = jax.random.split(key, 3)
    most = PPI * PAGE
    heavy = jax.random.randint(first, (REQ, N_INST), most // 2, most + 1)
    light = jax.random.randint(second, (REQ, N_INST), 1, most // 2 + 1)
    lower = (jnp.arange(N_INST) < N_INST // 2)[None, :]
    counts = jnp.where(lower, heavy, light)
    full = jax.random.randint(third, (REQ,), 0, N_INST)
    counts = jnp.where(jnp.arange(N_INST)[None, :] == full[:, None], most, counts)
    return counts.astype(jnp.int32)


def draw_move_slots(key, part):
    key = jax.random.fold_in(key, 41)
    inst_keys = jax.random.split(key, N_INST)
    chosen = jax.vmap(lambda sub: jax.random.permutation(sub, SLOTS)[:MOVES])(inst_keys)
    return chosen.astype(jnp.int32)


def steps_of(rng, dims, cuts, smallest, top_value):
    loudness = 1.0
    for axis_at, shards_of in cuts:
        draws = jax.random.uniform(jax.random.fold_in(jax.random.fold_in(rng, 6), axis_at), (shards_of,), jnp.float32, smallest / len(cuts), top_value / len(cuts))
        loudness = loudness * jnp.repeat(jnp.exp(draws), dims[axis_at] // shards_of).reshape((-1,) + (1,) * (len(dims) - 1 - axis_at))
    return loudness


def bell_draw(own_key, shape, width, most, cuts=(), kind=jnp.bfloat16):
    factor_of = steps_of(own_key, shape, cuts, -0.22, 0.18) if cuts else 1.0
    array = jax.random.normal(own_key, shape, jnp.float32) * width * factor_of
    return jnp.minimum(jnp.maximum(array, -most), most).astype(kind)


def setup_inputs(seed: int = 0) -> dict:
    key_list = jax.random.split(jax.random.key(seed), 7)
    return {
        "queries": draw_queries(jax.random.fold_in(key_list[6], 71), 0),
        "page_pool": draw_page_pool(jax.random.fold_in(key_list[6], 71), 0),
        "block_tables": draw_block_tables(jax.random.fold_in(key_list[6], 71), 0),
        "token_counts": draw_token_counts(jax.random.fold_in(key_list[6], 71), 0),
        "move_slots": draw_move_slots(jax.random.fold_in(key_list[6], 71), 0),
        "out_weight": bell_draw(key_list[5], (QH * HD, D), (QH * HD) ** -0.5, 0.046875, ((0, 16), (1, 16))),
    }


NEG_BIG = -1e30


def reference(queries, page_pool, block_tables, token_counts, move_slots, out_weight):
    group = QH // KVS
    score_scale = 1.0 / (HD ** 0.5)
    positions = jnp.arange(PPI, dtype=jnp.int32)[:, None] * PAGE + jnp.arange(PAGE, dtype=jnp.int32)[None, :]
    inst_rows = jnp.arange(N_INST, dtype=jnp.int32)

    def one_request(index):
        page_ids = (inst_rows[:, None] * SLOTS + block_tables[index]).astype(jnp.int32)
        pages = jnp.take(page_pool, page_ids, axis=0)
        page_keys = pages[:, :, 0].astype(jnp.float32)
        page_values = pages[:, :, 1].astype(jnp.float32)
        query_rows = queries[index].astype(jnp.float32).reshape(KVS, group, HD)
        scores = jnp.einsum("cgd,npctd->cgnpt", query_rows, page_keys) * score_scale
        token_live = positions[None, :, :] < token_counts[index][:, None, None]
        masked = jnp.where(token_live[None, None], scores, NEG_BIG)
        local_max = jnp.max(masked, axis=(3, 4))
        weights = jnp.exp(masked - local_max[..., None, None]).astype(jnp.bfloat16)
        wide = weights.astype(jnp.float32)
        local_sum = jnp.sum(wide, axis=(3, 4))
        local_out = jnp.einsum("cgnpt,npctd->cgnd", wide, page_values)
        top = jnp.max(local_max, axis=2)
        scaled = jnp.exp(local_max - top[..., None])
        numer = jnp.sum(scaled[..., None] * local_out, axis=2)
        denom = jnp.sum(scaled * local_sum, axis=2)
        return (numer / denom[..., None]).reshape(QH * HD).astype(jnp.bfloat16)

    attended = lax.map(one_request, jnp.arange(REQ, dtype=jnp.int32))
    projected = jnp.dot(attended, out_weight, preferred_element_type=jnp.float32).astype(jnp.bfloat16)
    sources = ((inst_rows + N_INST // 2) % N_INST).astype(jnp.int32)
    move_ids = (sources[:, None] * SLOTS + move_slots[sources]).astype(jnp.int32).reshape(N_INST * MOVES)
    arrived = jnp.take(page_pool, move_ids, axis=0)
    return projected, arrived
```

```python
import jax
import jax.numpy as jnp
from jax import lax
from jax.experimental import pallas as pl
from jax.experimental.pallas import tpu as pltpu
from jax.sharding import PartitionSpec as P

NEG_BIG = -1e30
STAT_ROWS = 16


def gather_pages(page_pool, move_slots, parity_axis, cuts):
    half = sum(cuts)
    firsts = [sum(cuts[:k]) for k in range(len(cuts))]

    def kernel(slots_ref, pool_ref, *rest):
        piece_refs, sems = rest[:-1], rest[-1]
        first = lax.rem(lax.axis_index(parity_axis), 2) * half
        moves = [
            pltpu.make_async_copy(
                pool_ref.at[slots_ref[0, first + at + k]], ref.at[k], sems.at[at + k]
            )
            for at, cut, ref in zip(firsts, cuts, piece_refs)
            for k in range(cut)
        ]
        for move in moves:
            move.start()
        for move in moves:
            move.wait()

    return pl.pallas_call(
        kernel,
        out_shape=[
            jax.ShapeDtypeStruct((cut,) + page_pool.shape[1:], page_pool.dtype) for cut in cuts
        ],
        in_specs=[
            pl.BlockSpec(memory_space=pltpu.SMEM),
            pl.BlockSpec(memory_space=pl.ANY),
        ],
        out_specs=[pl.BlockSpec(memory_space=pltpu.VMEM)] * len(cuts),
        scratch_shapes=[pltpu.SemaphoreType.DMA((half,))],
        compiler_params=pltpu.CompilerParams(vmem_limit_bytes=58 * 1024 * 1024),
        name="gather_pages",
    )(move_slots, page_pool)


def join_pieces(mine, theirs, parity_axis):
    cuts = [piece.shape[0] for piece in mine]
    half = sum(cuts)
    firsts = [sum(cuts[:k]) for k in range(len(cuts))]
    many = len(cuts)

    def kernel(*refs):
        mine_refs, theirs_refs = refs[:many], refs[many : 2 * many]
        out_ref, sems = refs[2 * many :]
        parity = lax.rem(lax.axis_index(parity_axis), 2)
        moves = []
        for side, pieces in ((parity, mine_refs), (1 - parity, theirs_refs)):
            for at, cut, ref in zip(firsts, cuts, pieces):
                rows = pl.ds(side * half + at, cut)
                moves.append(pltpu.make_async_copy(ref, out_ref.at[rows], sems.at[len(moves)]))
        for move in moves:
            move.start()
        for move in moves:
            move.wait()

    return pl.pallas_call(
        kernel,
        out_shape=jax.ShapeDtypeStruct((2 * half,) + mine[0].shape[1:], mine[0].dtype),
        in_specs=[pl.BlockSpec(memory_space=pltpu.VMEM)] * (2 * many),
        out_specs=pl.BlockSpec(memory_space=pl.ANY),
        scratch_shapes=[pltpu.SemaphoreType.DMA((2 * many,))],
        compiler_params=pltpu.CompilerParams(vmem_limit_bytes=4 * 1024 * 1024),
        name="join_pieces",
    )(*mine, *theirs)


def attend(queries, page_pool, block_tables, token_counts):
    requests, heads, size = queries.shape
    pages = block_tables.shape[1]
    page_len = page_pool.shape[3]
    tokens = pages * page_len
    rows = requests * heads
    scale = 1.0 / size**0.5

    def kernel(tables_ref, counts_ref, queries_ref, pool_ref, out_ref, query_ref, score_ref):
        for r in range(requests):
            query_ref[pl.ds(r, heads, stride=requests), :] = queries_ref[r].astype(jnp.float32)
        turned = jnp.transpose(query_ref[...]).astype(jnp.bfloat16)
        lane = lax.rem(lax.broadcasted_iota(jnp.int32, (1, rows), 1), requests)
        limit = jnp.zeros((1, rows), jnp.int32)
        for r in range(requests):
            limit = jnp.where(lane == r, counts_ref[r], limit)
        for r in range(requests):
            keys = jnp.concatenate([pool_ref[tables_ref[r, j], 0, 0] for j in range(pages)], axis=0)
            tile = jnp.dot(keys, turned, preferred_element_type=jnp.float32)
            score_ref[...] = tile if r == 0 else jnp.where(lane == r, tile, score_ref[...])
        position = lax.broadcasted_iota(jnp.int32, (tokens, rows), 0)
        scores = jnp.where(position < limit, score_ref[...] * scale, NEG_BIG)
        top = jnp.max(scores, axis=0, keepdims=True)
        weights = jnp.exp(scores - top).astype(jnp.bfloat16)
        total = jnp.sum(weights.astype(jnp.float32), axis=0, keepdims=True)
        weights = jnp.transpose(weights)
        row = lax.rem(lax.broadcasted_iota(jnp.int32, (rows, size), 0), requests)
        out = jnp.zeros((rows, size), jnp.float32)
        for r in range(requests):
            values = jnp.concatenate(
                [pool_ref[tables_ref[r, j], 1, 0] for j in range(pages)], axis=0
            )
            share = jnp.dot(weights, values, preferred_element_type=jnp.float32)
            out = jnp.where(row == r, share, out)
        out_ref[pl.ds(0, rows), :] = out / jnp.transpose(jnp.broadcast_to(total, (rows, rows)))
        out_ref[pl.ds(rows, 8), :] = jnp.broadcast_to(top + jnp.log(total), (8, rows))

    return pl.pallas_call(
        kernel,
        out_shape=jax.ShapeDtypeStruct((rows + 8, size), jnp.float32),
        in_specs=[
            pl.BlockSpec(memory_space=pltpu.SMEM),
            pl.BlockSpec(memory_space=pltpu.SMEM),
            pl.BlockSpec(memory_space=pltpu.VMEM),
            pl.BlockSpec(memory_space=pltpu.VMEM),
        ],
        out_specs=pl.BlockSpec(memory_space=pltpu.VMEM),
        scratch_shapes=[
            pltpu.VMEM((rows, size), jnp.float32),
            pltpu.VMEM((tokens, rows), jnp.float32),
        ],
        compiler_params=pltpu.CompilerParams(vmem_limit_bytes=16 * 1024 * 1024),
        name="attend",
    )(block_tables, token_counts, queries, page_pool)


def merge_two(mine, theirs, copies):
    rows, size = mine.shape[0] - 8, mine.shape[1]

    def kernel(mine_ref, theirs_ref, out_ref):
        log_one = mine_ref[pl.ds(rows, 1), :]
        log_two = theirs_ref[pl.ds(rows, 1), :]
        top = jnp.maximum(log_one, log_two)
        one = jnp.exp(log_one - top)
        two = jnp.exp(log_two - top)
        total = one + two
        logs = top + jnp.log(total)
        weight = jnp.transpose(jnp.broadcast_to(one / total, (rows, rows)))
        other = jnp.transpose(jnp.broadcast_to(two / total, (rows, rows)))
        parts = weight * mine_ref[pl.ds(0, rows), :] + other * theirs_ref[pl.ds(0, rows), :]
        high = logs.astype(jnp.bfloat16).astype(jnp.float32)
        middle = (logs - high).astype(jnp.bfloat16).astype(jnp.float32)
        low = logs - high - middle
        row = lax.broadcasted_iota(jnp.int32, (STAT_ROWS, rows), 0)
        stats = jnp.where(row == 0, high, jnp.where(row == 1, middle, jnp.where(row == 2, low, 0.0)))
        parts = parts.astype(jnp.bfloat16)
        stats = stats.astype(jnp.bfloat16)
        for i in range(copies):
            out_ref[i, pl.ds(0, rows), :] = parts
            out_ref[i, pl.ds(rows, STAT_ROWS), :] = stats

    return pl.pallas_call(
        kernel,
        out_shape=jax.ShapeDtypeStruct((copies, rows + STAT_ROWS, size), jnp.bfloat16),
        in_specs=[pl.BlockSpec(memory_space=pltpu.VMEM)] * 2,
        out_specs=pl.BlockSpec(memory_space=pltpu.VMEM),
        compiler_params=pltpu.CompilerParams(vmem_limit_bytes=4 * 1024 * 1024),
        name="merge_two",
    )(mine, theirs)


def combine_and_project(parts, out_weight, requests, heads):
    sources, _, size = parts.shape
    rows = requests * heads
    columns = out_weight.shape[1]
    folds = columns // size

    def kernel(parts_ref, weight_ref, out_ref):
        stats = parts_ref[:, pl.ds(rows, STAT_ROWS), :].astype(jnp.float32)
        logs = stats[:, 0, :] + stats[:, 1, :] + stats[:, 2, :]
        share = jnp.exp(logs - jnp.max(logs, axis=0, keepdims=True))
        share = share / jnp.sum(share, axis=0, keepdims=True)
        share = jnp.transpose(share)
        total = jnp.zeros((rows, size), jnp.float32)
        for i in range(sources):
            total += share[:, i : i + 1] * parts_ref[i, pl.ds(0, rows), :].astype(jnp.float32)
        attended = total.astype(jnp.bfloat16)
        attended = jnp.concatenate(
            [attended[h * requests : (h + 1) * requests] for h in range(heads)], axis=1
        )
        terms = jnp.dot(attended, weight_ref[...], preferred_element_type=jnp.float32)
        for c in range(folds):
            out_ref[pl.ds(c, requests, stride=folds), :] = terms[:, c * size : (c + 1) * size]

    return pl.pallas_call(
        kernel,
        out_shape=jax.ShapeDtypeStruct((requests * folds, size), jnp.float32),
        in_specs=[pl.BlockSpec(memory_space=pltpu.VMEM)] * 2,
        out_specs=pl.BlockSpec(memory_space=pltpu.VMEM),
        compiler_params=pltpu.CompilerParams(vmem_limit_bytes=16 * 1024 * 1024),
        name="combine_and_project",
    )(parts, out_weight)


def sum_terms(terms):
    _, folds, size = terms.shape

    def kernel(terms_ref, out_ref):
        total = jnp.sum(terms_ref[...], axis=0).astype(jnp.bfloat16)
        for c in range(folds):
            out_ref[:, pl.ds(c * size, size)] = total[c : c + 1, :]

    return pl.pallas_call(
        kernel,
        out_shape=jax.ShapeDtypeStruct((1, folds * size), jnp.bfloat16),
        in_specs=[pl.BlockSpec(memory_space=pltpu.VMEM)],
        out_specs=pl.BlockSpec(memory_space=pltpu.VMEM),
        compiler_params=pltpu.CompilerParams(vmem_limit_bytes=2 * 1024 * 1024),
        name="sum_terms",
    )(terms)


def body(queries, page_pool, block_tables, token_counts, move_slots, out_weight):
    instances = lax.axis_size("inst")
    devices = lax.axis_size("head")
    heads, size = queries.shape[1:]
    requests = instances * queries.shape[0]

    half = move_slots.shape[1] // 2
    cuts = (half - half // 2, half // 2)
    far = [(i, (i + instances // 2) % instances) for i in range(instances)]
    side = [(i, i ^ 1) for i in range(instances)]
    pair = [(i, i ^ 1) for i in range(devices)]
    rings = [[2 * k + s for k in range(instances // 2)] for s in range(2)]

    copies = jnp.broadcast_to(queries, (instances, heads, size))
    all_queries = lax.all_to_all(copies, "inst", 0, 0, tiled=True)
    first, second = gather_pages(page_pool, move_slots, "head", cuts)

    first, all_queries = lax.optimization_barrier((first, all_queries))
    first = lax.ppermute(first, "inst", far)
    parts = attend(all_queries, page_pool, block_tables[:, 0, :], token_counts[:, 0])
    others = lax.ppermute(parts, "inst", side)
    parts = merge_two(parts, others, instances // 2)
    first, parts = lax.optimization_barrier((first, parts))
    first_too = lax.ppermute(first, "head", pair)
    parts = lax.all_to_all(parts, "inst", 0, 0, tiled=True, axis_index_groups=rings)

    second, parts = lax.optimization_barrier((second, parts))
    second = lax.ppermute(second, "inst", far)
    terms = combine_and_project(parts, out_weight, requests, heads)
    terms = terms.reshape(devices, terms.shape[0] // devices, size)
    terms = lax.all_to_all(terms, "head", 0, 0, tiled=True)
    second, terms = lax.optimization_barrier((second, terms))
    second_too = lax.ppermute(second, "head", pair)
    arrived = join_pieces((first, second), (first_too, second_too), "head")
    return (sum_terms(terms), arrived)


def solution(mesh):
    in_specs = (
        P("inst", "head", None),
        P("inst", None, "head", None, None),
        P(None, "inst", None),
        P(None, "inst"),
        P("inst", None),
        P("head", "inst"),
    )
    out_specs = (P("head", "inst"), P("inst", None, "head", None, None))
    return jax.shard_map(body, mesh=mesh, in_specs=in_specs, out_specs=out_specs, check_vma=False)
```

```python
import jax
import jax.numpy as jnp
from jax import lax
from jax.experimental import pallas as pl
from jax.experimental.pallas import tpu as pltpu
from jax.sharding import PartitionSpec as P

NEG_BIG = -1e30
STAT_ROWS = 16


def gather_pages(page_pool, move_slots, parity_axis, cuts):
    half = sum(cuts)
    firsts = [sum(cuts[:k]) for k in range(len(cuts))]

    def kernel(slots_ref, pool_ref, *rest):
        piece_refs, sems = rest[:-1], rest[-1]
        first = lax.rem(lax.axis_index(parity_axis), 2) * half
        moves = [
            pltpu.make_async_copy(
                pool_ref.at[slots_ref[0, first + at + k]], ref.at[k], sems.at[at + k]
            )
            for at, cut, ref in zip(firsts, cuts, piece_refs)
            for k in range(cut)
        ]
        for move in moves:
            move.start()
        for move in moves:
            move.wait()

    return pl.pallas_call(
        kernel,
        out_shape=[
            jax.ShapeDtypeStruct((cut,) + page_pool.shape[1:], page_pool.dtype) for cut in cuts
        ],
        in_specs=[
            pl.BlockSpec(memory_space=pltpu.SMEM),
            pl.BlockSpec(memory_space=pl.ANY),
        ],
        out_specs=[pl.BlockSpec(memory_space=pltpu.VMEM)] * len(cuts),
        scratch_shapes=[pltpu.SemaphoreType.DMA((half,))],
        compiler_params=pltpu.CompilerParams(vmem_limit_bytes=58 * 1024 * 1024),
        name="gather_pages",
    )(move_slots, page_pool)


def join_pieces(mine, theirs, parity_axis):
    cuts = [piece.shape[0] for piece in mine]
    half = sum(cuts)
    firsts = [sum(cuts[:k]) for k in range(len(cuts))]
    many = len(cuts)

    def kernel(*refs):
        mine_refs, theirs_refs = refs[:many], refs[many : 2 * many]
        out_ref, sems = refs[2 * many :]
        parity = lax.rem(lax.axis_index(parity_axis), 2)
        moves = []
        for side, pieces in ((parity, mine_refs), (1 - parity, theirs_refs)):
            for at, cut, ref in zip(firsts, cuts, pieces):
                rows = pl.ds(side * half + at, cut)
                moves.append(pltpu.make_async_copy(ref, out_ref.at[rows], sems.at[len(moves)]))
        for move in moves:
            move.start()
        for move in moves:
            move.wait()

    return pl.pallas_call(
        kernel,
        out_shape=jax.ShapeDtypeStruct((2 * half,) + mine[0].shape[1:], mine[0].dtype),
        in_specs=[pl.BlockSpec(memory_space=pltpu.VMEM)] * (2 * many),
        out_specs=pl.BlockSpec(memory_space=pl.ANY),
        scratch_shapes=[pltpu.SemaphoreType.DMA((2 * many,))],
        compiler_params=pltpu.CompilerParams(vmem_limit_bytes=4 * 1024 * 1024),
        name="join_pieces",
    )(*mine, *theirs)


def attend(queries, page_pool, block_tables, token_counts):
    requests, heads, size = queries.shape
    pages = block_tables.shape[1]
    page_len = page_pool.shape[3]
    tokens = pages * page_len
    rows = requests * heads
    scale = 1.0 / size**0.5

    def kernel(tables_ref, counts_ref, queries_ref, pool_ref, out_ref, query_ref, score_ref):
        for r in range(requests):
            query_ref[pl.ds(r, heads, stride=requests), :] = queries_ref[r].astype(jnp.float32)
        turned = jnp.transpose(query_ref[...]).astype(jnp.bfloat16)
        lane = lax.rem(lax.broadcasted_iota(jnp.int32, (1, rows), 1), requests)
        limit = jnp.zeros((1, rows), jnp.int32)
        for r in range(requests):
            limit = jnp.where(lane == r, counts_ref[r], limit)
        for r in range(requests):
            keys = jnp.concatenate([pool_ref[tables_ref[r, j], 0, 0] for j in range(pages)], axis=0)
            tile = jnp.dot(keys, turned, preferred_element_type=jnp.float32)
            score_ref[...] = tile if r == 0 else jnp.where(lane == r, tile, score_ref[...])
        position = lax.broadcasted_iota(jnp.int32, (tokens, rows), 0)
        scores = jnp.where(position < limit, score_ref[...] * scale, NEG_BIG)
        top = jnp.max(scores, axis=0, keepdims=True)
        weights = jnp.exp(scores - top).astype(jnp.bfloat16)
        total = jnp.sum(weights.astype(jnp.float32), axis=0, keepdims=True)
        weights = jnp.transpose(weights)
        row = lax.rem(lax.broadcasted_iota(jnp.int32, (rows, size), 0), requests)
        out = jnp.zeros((rows, size), jnp.float32)
        for r in range(requests):
            values = jnp.concatenate(
                [pool_ref[tables_ref[r, j], 1, 0] for j in range(pages)], axis=0
            )
            share = jnp.dot(weights, values, preferred_element_type=jnp.float32)
            out = jnp.where(row == r, share, out)
        out_ref[pl.ds(0, rows), :] = out / jnp.transpose(jnp.broadcast_to(total, (rows, rows)))
        out_ref[pl.ds(rows, 8), :] = jnp.broadcast_to(top + jnp.log(total), (8, rows))

    return pl.pallas_call(
        kernel,
        out_shape=jax.ShapeDtypeStruct((rows + 8, size), jnp.float32),
        in_specs=[
            pl.BlockSpec(memory_space=pltpu.SMEM),
            pl.BlockSpec(memory_space=pltpu.SMEM),
            pl.BlockSpec(memory_space=pltpu.VMEM),
            pl.BlockSpec(memory_space=pltpu.VMEM),
        ],
        out_specs=pl.BlockSpec(memory_space=pltpu.VMEM),
        scratch_shapes=[
            pltpu.VMEM((rows, size), jnp.float32),
            pltpu.VMEM((tokens, rows), jnp.float32),
        ],
        compiler_params=pltpu.CompilerParams(vmem_limit_bytes=16 * 1024 * 1024),
        name="attend",
    )(block_tables, token_counts, queries, page_pool)


def merge_two(mine, theirs, copies):
    rows, size = mine.shape[0] - 8, mine.shape[1]

    def kernel(mine_ref, theirs_ref, out_ref):
        log_one = mine_ref[pl.ds(rows, 1), :]
        log_two = theirs_ref[pl.ds(rows, 1), :]
        top = jnp.maximum(log_one, log_two)
        one = jnp.exp(log_one - top)
        two = jnp.exp(log_two - top)
        total = one + two
        logs = top + jnp.log(total)
        weight = jnp.transpose(jnp.broadcast_to(one / total, (rows, rows)))
        other = jnp.transpose(jnp.broadcast_to(two / total, (rows, rows)))
        parts = weight * mine_ref[pl.ds(0, rows), :] + other * theirs_ref[pl.ds(0, rows), :]
        high = logs.astype(jnp.bfloat16).astype(jnp.float32)
        middle = (logs - high).astype(jnp.bfloat16).astype(jnp.float32)
        low = logs - high - middle
        row = lax.broadcasted_iota(jnp.int32, (STAT_ROWS, rows), 0)
        stats = jnp.where(row == 0, high, jnp.where(row == 1, middle, jnp.where(row == 2, low, 0.0)))
        parts = parts.astype(jnp.bfloat16)
        stats = stats.astype(jnp.bfloat16)
        for i in range(copies):
            out_ref[i, pl.ds(0, rows), :] = parts
            out_ref[i, pl.ds(rows, STAT_ROWS), :] = stats

    return pl.pallas_call(
        kernel,
        out_shape=jax.ShapeDtypeStruct((copies, rows + STAT_ROWS, size), jnp.bfloat16),
        in_specs=[pl.BlockSpec(memory_space=pltpu.VMEM)] * 2,
        out_specs=pl.BlockSpec(memory_space=pltpu.VMEM),
        compiler_params=pltpu.CompilerParams(vmem_limit_bytes=4 * 1024 * 1024),
        name="merge_two",
    )(mine, theirs)


def combine_and_project(parts, out_weight, requests, heads):
    sources, _, size = parts.shape
    rows = requests * heads
    columns = out_weight.shape[1]
    folds = columns // size

    def kernel(parts_ref, weight_ref, out_ref):
        stats = parts_ref[:, pl.ds(rows, STAT_ROWS), :].astype(jnp.float32)
        logs = stats[:, 0, :] + stats[:, 1, :] + stats[:, 2, :]
        share = jnp.exp(logs - jnp.max(logs, axis=0, keepdims=True))
        share = share / jnp.sum(share, axis=0, keepdims=True)
        share = jnp.transpose(share)
        total = jnp.zeros((rows, size), jnp.float32)
        for i in range(sources):
            total += share[:, i : i + 1] * parts_ref[i, pl.ds(0, rows), :].astype(jnp.float32)
        attended = total.astype(jnp.bfloat16)
        attended = jnp.concatenate(
            [attended[h * requests : (h + 1) * requests] for h in range(heads)], axis=1
        )
        terms = jnp.dot(attended, weight_ref[...], preferred_element_type=jnp.float32)
        for c in range(folds):
            out_ref[pl.ds(c, requests, stride=folds), :] = terms[:, c * size : (c + 1) * size]

    return pl.pallas_call(
        kernel,
        out_shape=jax.ShapeDtypeStruct((requests * folds, size), jnp.float32),
        in_specs=[pl.BlockSpec(memory_space=pltpu.VMEM)] * 2,
        out_specs=pl.BlockSpec(memory_space=pltpu.VMEM),
        compiler_params=pltpu.CompilerParams(vmem_limit_bytes=16 * 1024 * 1024),
        name="combine_and_project",
    )(parts, out_weight)


def sum_terms(terms):
    _, folds, size = terms.shape

    def kernel(terms_ref, out_ref):
        total = jnp.sum(terms_ref[...], axis=0).astype(jnp.bfloat16)
        for c in range(folds):
            out_ref[:, pl.ds(c * size, size)] = total[c : c + 1, :]

    return pl.pallas_call(
        kernel,
        out_shape=jax.ShapeDtypeStruct((1, folds * size), jnp.bfloat16),
        in_specs=[pl.BlockSpec(memory_space=pltpu.VMEM)],
        out_specs=pl.BlockSpec(memory_space=pltpu.VMEM),
        compiler_params=pltpu.CompilerParams(vmem_limit_bytes=2 * 1024 * 1024),
        name="sum_terms",
    )(terms)


def body(queries, page_pool, block_tables, token_counts, move_slots, out_weight):
    instances = lax.axis_size("inst")
    devices = lax.axis_size("head")
    heads, size = queries.shape[1:]
    requests = instances * queries.shape[0]

    half = move_slots.shape[1] // 2
    cuts = (half - half // 2, half // 2)
    far = [(i, (i + instances // 2) % instances) for i in range(instances)]
    side = [(i, i ^ 1) for i in range(instances)]
    pair = [(i, i ^ 1) for i in range(devices)]
    rings = [[2 * k + s for k in range(instances // 2)] for s in range(2)]

    copies = jnp.broadcast_to(queries, (instances, heads, size))
    all_queries = lax.all_to_all(copies, "inst", 0, 0, tiled=True)
    first, second = gather_pages(page_pool, move_slots, "head", cuts)

    first, all_queries = lax.optimization_barrier((first, all_queries))
    first = lax.ppermute(first, "inst", far)
    parts = attend(all_queries, page_pool, block_tables[:, 0, :], token_counts[:, 0])
    others = lax.ppermute(parts, "inst", side)
    parts = merge_two(parts, others, instances // 2)
    first, parts = lax.optimization_barrier((first, parts))
    first_too = lax.ppermute(first, "head", pair)
    parts = lax.all_to_all(parts, "inst", 0, 0, tiled=True, axis_index_groups=rings)

    terms = combine_and_project(parts, out_weight, requests, heads)
    terms = terms.reshape(devices, terms.shape[0] // devices, size)
    second, terms = lax.optimization_barrier((second, terms))
    second = lax.ppermute(second, "inst", far)
    terms = lax.all_to_all(terms, "head", 0, 0, tiled=True)
    second, terms = lax.optimization_barrier((second, terms))
    second_too = lax.ppermute(second, "head", pair)
    arrived = join_pieces((first, second), (first_too, second_too), "head")
    return (sum_terms(terms), arrived)


def solution(mesh):
    in_specs = (
        P("inst", "head", None),
        P("inst", None, "head", None, None),
        P(None, "inst", None),
        P(None, "inst"),
        P("inst", None),
        P("head", "inst"),
    )
    out_specs = (P("head", "inst"), P("inst", None, "head", None, None))
    return jax.shard_map(body, mesh=mesh, in_specs=in_specs, out_specs=out_specs, check_vma=False)
```

```python
import jax
import jax.numpy as jnp
from jax import lax
from jax.experimental import pallas as pl
from jax.experimental.pallas import tpu as pltpu
from jax.sharding import PartitionSpec as P

NEG_BIG = -1e30
STAT_ROWS = 16


def gather_pages(page_pool, move_slots, parity_axis, cuts):
    half = sum(cuts)
    firsts = [sum(cuts[:k]) for k in range(len(cuts))]

    def kernel(slots_ref, pool_ref, *rest):
        piece_refs, sems = rest[:-1], rest[-1]
        first = lax.rem(lax.axis_index(parity_axis), 2) * half
        moves = [
            pltpu.make_async_copy(
                pool_ref.at[slots_ref[0, first + at + k]], ref.at[k], sems.at[at + k]
            )
            for at, cut, ref in zip(firsts, cuts, piece_refs)
            for k in range(cut)
        ]
        for move in moves:
            move.start()
        for move in moves:
            move.wait()

    return pl.pallas_call(
        kernel,
        out_shape=[
            jax.ShapeDtypeStruct((cut,) + page_pool.shape[1:], page_pool.dtype) for cut in cuts
        ],
        in_specs=[
            pl.BlockSpec(memory_space=pltpu.SMEM),
            pl.BlockSpec(memory_space=pl.ANY),
        ],
        out_specs=[pl.BlockSpec(memory_space=pltpu.VMEM)] * len(cuts),
        scratch_shapes=[pltpu.SemaphoreType.DMA((half,))],
        compiler_params=pltpu.CompilerParams(vmem_limit_bytes=58 * 1024 * 1024),
        name="gather_pages",
    )(move_slots, page_pool)


def join_pieces(mine, theirs, parity_axis):
    cuts = [piece.shape[0] for piece in mine]
    half = sum(cuts)
    firsts = [sum(cuts[:k]) for k in range(len(cuts))]
    many = len(cuts)

    def kernel(*refs):
        mine_refs, theirs_refs = refs[:many], refs[many : 2 * many]
        out_ref, sems = refs[2 * many :]
        parity = lax.rem(lax.axis_index(parity_axis), 2)
        moves = []
        for side, pieces in ((parity, mine_refs), (1 - parity, theirs_refs)):
            for at, cut, ref in zip(firsts, cuts, pieces):
                rows = pl.ds(side * half + at, cut)
                moves.append(pltpu.make_async_copy(ref, out_ref.at[rows], sems.at[len(moves)]))
        for move in moves:
            move.start()
        for move in moves:
            move.wait()

    return pl.pallas_call(
        kernel,
        out_shape=jax.ShapeDtypeStruct((2 * half,) + mine[0].shape[1:], mine[0].dtype),
        in_specs=[pl.BlockSpec(memory_space=pltpu.VMEM)] * (2 * many),
        out_specs=pl.BlockSpec(memory_space=pl.ANY),
        scratch_shapes=[pltpu.SemaphoreType.DMA((2 * many,))],
        compiler_params=pltpu.CompilerParams(vmem_limit_bytes=4 * 1024 * 1024),
        name="join_pieces",
    )(*mine, *theirs)


def attend(queries, page_pool, block_tables, token_counts):
    requests, heads, size = queries.shape
    pages = block_tables.shape[1]
    page_len = page_pool.shape[3]
    tokens = pages * page_len
    rows = requests * heads
    scale = 1.0 / size**0.5

    def kernel(tables_ref, counts_ref, queries_ref, pool_ref, out_ref, query_ref, score_ref):
        for r in range(requests):
            query_ref[pl.ds(r, heads, stride=requests), :] = queries_ref[r].astype(jnp.float32)
        turned = jnp.transpose(query_ref[...]).astype(jnp.bfloat16)
        lane = lax.rem(lax.broadcasted_iota(jnp.int32, (1, rows), 1), requests)
        limit = jnp.zeros((1, rows), jnp.int32)
        for r in range(requests):
            limit = jnp.where(lane == r, counts_ref[r], limit)
        for r in range(requests):
            keys = jnp.concatenate([pool_ref[tables_ref[r, j], 0, 0] for j in range(pages)], axis=0)
            tile = jnp.dot(keys, turned, preferred_element_type=jnp.float32)
            score_ref[...] = tile if r == 0 else jnp.where(lane == r, tile, score_ref[...])
        position = lax.broadcasted_iota(jnp.int32, (tokens, rows), 0)
        scores = jnp.where(position < limit, score_ref[...] * scale, NEG_BIG)
        top = jnp.max(scores, axis=0, keepdims=True)
        weights = jnp.exp(scores - top).astype(jnp.bfloat16)
        total = jnp.sum(weights.astype(jnp.float32), axis=0, keepdims=True)
        weights = jnp.transpose(weights)
        row = lax.rem(lax.broadcasted_iota(jnp.int32, (rows, size), 0), requests)
        out = jnp.zeros((rows, size), jnp.float32)
        for r in range(requests):
            values = jnp.concatenate(
                [pool_ref[tables_ref[r, j], 1, 0] for j in range(pages)], axis=0
            )
            share = jnp.dot(weights, values, preferred_element_type=jnp.float32)
            out = jnp.where(row == r, share, out)
        out_ref[pl.ds(0, rows), :] = out / jnp.transpose(jnp.broadcast_to(total, (rows, rows)))
        out_ref[pl.ds(rows, 8), :] = jnp.broadcast_to(top + jnp.log(total), (8, rows))

    return pl.pallas_call(
        kernel,
        out_shape=jax.ShapeDtypeStruct((rows + 8, size), jnp.float32),
        in_specs=[
            pl.BlockSpec(memory_space=pltpu.SMEM),
            pl.BlockSpec(memory_space=pltpu.SMEM),
            pl.BlockSpec(memory_space=pltpu.VMEM),
            pl.BlockSpec(memory_space=pltpu.VMEM),
        ],
        out_specs=pl.BlockSpec(memory_space=pltpu.VMEM),
        scratch_shapes=[
            pltpu.VMEM((rows, size), jnp.float32),
            pltpu.VMEM((tokens, rows), jnp.float32),
        ],
        compiler_params=pltpu.CompilerParams(vmem_limit_bytes=16 * 1024 * 1024),
        name="attend",
    )(block_tables, token_counts, queries, page_pool)


def merge_two(mine, theirs, copies):
    rows, size = mine.shape[0] - 8, mine.shape[1]

    def kernel(mine_ref, theirs_ref, out_ref):
        log_one = mine_ref[pl.ds(rows, 1), :]
        log_two = theirs_ref[pl.ds(rows, 1), :]
        top = jnp.maximum(log_one, log_two)
        one = jnp.exp(log_one - top)
        two = jnp.exp(log_two - top)
        total = one + two
        logs = top + jnp.log(total)
        weight = jnp.transpose(jnp.broadcast_to(one / total, (rows, rows)))
        other = jnp.transpose(jnp.broadcast_to(two / total, (rows, rows)))
        parts = weight * mine_ref[pl.ds(0, rows), :] + other * theirs_ref[pl.ds(0, rows), :]
        high = logs.astype(jnp.bfloat16).astype(jnp.float32)
        middle = (logs - high).astype(jnp.bfloat16).astype(jnp.float32)
        low = logs - high - middle
        row = lax.broadcasted_iota(jnp.int32, (STAT_ROWS, rows), 0)
        stats = jnp.where(row == 0, high, jnp.where(row == 1, middle, jnp.where(row == 2, low, 0.0)))
        parts = parts.astype(jnp.bfloat16)
        stats = stats.astype(jnp.bfloat16)
        for i in range(copies):
            out_ref[i, pl.ds(0, rows), :] = parts
            out_ref[i, pl.ds(rows, STAT_ROWS), :] = stats

    return pl.pallas_call(
        kernel,
        out_shape=jax.ShapeDtypeStruct((copies, rows + STAT_ROWS, size), jnp.bfloat16),
        in_specs=[pl.BlockSpec(memory_space=pltpu.VMEM)] * 2,
        out_specs=pl.BlockSpec(memory_space=pltpu.VMEM),
        compiler_params=pltpu.CompilerParams(vmem_limit_bytes=4 * 1024 * 1024),
        name="merge_two",
    )(mine, theirs)


def combine_and_project(parts, out_weight, requests, heads):
    sources, _, size = parts.shape
    rows = requests * heads
    columns = out_weight.shape[1]
    folds = columns // size

    def kernel(parts_ref, weight_ref, out_ref):
        stats = parts_ref[:, pl.ds(rows, STAT_ROWS), :].astype(jnp.float32)
        logs = stats[:, 0, :] + stats[:, 1, :] + stats[:, 2, :]
        share = jnp.exp(logs - jnp.max(logs, axis=0, keepdims=True))
        share = share / jnp.sum(share, axis=0, keepdims=True)
        share = jnp.transpose(share)
        total = jnp.zeros((rows, size), jnp.float32)
        for i in range(sources):
            total += share[:, i : i + 1] * parts_ref[i, pl.ds(0, rows), :].astype(jnp.float32)
        attended = total.astype(jnp.bfloat16)
        attended = jnp.concatenate(
            [attended[h * requests : (h + 1) * requests] for h in range(heads)], axis=1
        )
        terms = jnp.dot(attended, weight_ref[...], preferred_element_type=jnp.float32)
        for c in range(folds):
            out_ref[pl.ds(c, requests, stride=folds), :] = terms[:, c * size : (c + 1) * size]

    return pl.pallas_call(
        kernel,
        out_shape=jax.ShapeDtypeStruct((requests * folds, size), jnp.float32),
        in_specs=[pl.BlockSpec(memory_space=pltpu.VMEM)] * 2,
        out_specs=pl.BlockSpec(memory_space=pltpu.VMEM),
        compiler_params=pltpu.CompilerParams(vmem_limit_bytes=16 * 1024 * 1024),
        name="combine_and_project",
    )(parts, out_weight)


def sum_terms(terms):
    _, folds, size = terms.shape

    def kernel(terms_ref, out_ref):
        total = jnp.sum(terms_ref[...], axis=0).astype(jnp.bfloat16)
        for c in range(folds):
            out_ref[:, pl.ds(c * size, size)] = total[c : c + 1, :]

    return pl.pallas_call(
        kernel,
        out_shape=jax.ShapeDtypeStruct((1, folds * size), jnp.bfloat16),
        in_specs=[pl.BlockSpec(memory_space=pltpu.VMEM)],
        out_specs=pl.BlockSpec(memory_space=pltpu.VMEM),
        compiler_params=pltpu.CompilerParams(vmem_limit_bytes=2 * 1024 * 1024),
        name="sum_terms",
    )(terms)


def body(queries, page_pool, block_tables, token_counts, move_slots, out_weight):
    instances = lax.axis_size("inst")
    devices = lax.axis_size("head")
    heads, size = queries.shape[1:]
    requests = instances * queries.shape[0]

    half = move_slots.shape[1] // 2
    cuts = (half - half * 7 // 16, half * 7 // 16)
    far = [(i, (i + instances // 2) % instances) for i in range(instances)]
    side = [(i, i ^ 1) for i in range(instances)]
    pair = [(i, i ^ 1) for i in range(devices)]
    rings = [[2 * k + s for k in range(instances // 2)] for s in range(2)]

    copies = jnp.broadcast_to(queries, (instances, heads, size))
    all_queries = lax.all_to_all(copies, "inst", 0, 0, tiled=True)
    first, second = gather_pages(page_pool, move_slots, "head", cuts)

    first, all_queries = lax.optimization_barrier((first, all_queries))
    first = lax.ppermute(first, "inst", far)
    parts = attend(all_queries, page_pool, block_tables[:, 0, :], token_counts[:, 0])
    others = lax.ppermute(parts, "inst", side)
    parts = merge_two(parts, others, instances // 2)
    first, parts = lax.optimization_barrier((first, parts))
    first_too = lax.ppermute(first, "head", pair)
    parts = lax.all_to_all(parts, "inst", 0, 0, tiled=True, axis_index_groups=rings)

    second, parts = lax.optimization_barrier((second, parts))
    second = lax.ppermute(second, "inst", far)
    terms = combine_and_project(parts, out_weight, requests, heads)
    terms = terms.reshape(devices, terms.shape[0] // devices, size)
    terms = lax.all_to_all(terms, "head", 0, 0, tiled=True)
    second, terms = lax.optimization_barrier((second, terms))
    second_too = lax.ppermute(second, "head", pair)
    arrived = join_pieces((first, second), (first_too, second_too), "head")
    return (sum_terms(terms), arrived)


def solution(mesh):
    in_specs = (
        P("inst", "head", None),
        P("inst", None, "head", None, None),
        P(None, "inst", None),
        P(None, "inst"),
        P("inst", None),
        P("head", "inst"),
    )
    out_specs = (P("head", "inst"), P("inst", None, "head", None, None))
    return jax.shard_map(body, mesh=mesh, in_specs=in_specs, out_specs=out_specs, check_vma=False)
```
